512 devices in a mesh: dp: 32 (over z, y_hi), node: 16 (over y_lo, x, core).
Axes of the slice: x: 4, y: 4 (y_hi: 2, y_lo: 2; y = y_hi * 2 + y_lo), z: 16, core: 2. Of those that a mesh axis runs over, the one named last changes fastest.
Arguments:
- tokens_in: bfloat16 [32768, 4096], P('dp', 'node'), may hold values from -6 to 6
- out_grads: bfloat16 [32768, 4096], P('dp'), may hold values from -0.0078125 to 0.0078125
- left_old: float32 [4096, 4096], P('node', 'dp'), may hold values from -0.1 to 4.1, as said below
- right_old: float32 [4096, 4096], P('node', 'dp'), may hold values from -0.1 to 4.1, as said below
Outputs:
- left_out: float32 [4096, 4096], P('node', 'dp')
- right_out: float32 [4096, 4096], P('node', 'dp')
The draws below stay inside these ranges and needn't reach their ends.
Inputs may be any that keep to these rules, and one draw needn't show every extreme that they name: `left_old`: symmetric. `right_old`: symmetric.
All inputs are finite; a program needn't handle non-finite values.
Results may differ from the reference program's by a relative error of at most 0.0021.
Values may be sent and summed in bfloat16 or wider, within the bound.
A program may use at most 64 MiB of HBM per device.

```python
import jax
import jax.numpy as jnp

BLOCK = 4096
TOKENS = 32768


def symmetric_statistic(key, spread):
    noise_key, diagonal_key = jax.random.split(key)
    noise_field = jax.random.uniform(noise_key, (BLOCK, BLOCK), jnp.float32, -0.1, 0.1)
    symmetric = (noise_field + noise_field.T) * 0.5
    diagonal = jnp.exp(jax.random.uniform(diagonal_key, (BLOCK,), jnp.float32, 0.0, spread))
    return symmetric + jnp.eye(BLOCK, dtype=jnp.float32) * diagonal[None, :]


def draw_left_old(key, part):
    key = jax.random.fold_in(key, 11)
    return symmetric_statistic(key, 1.386)


def draw_right_old(key, part):
    key = jax.random.fold_in(key, 23)
    return symmetric_statistic(key, 1.386)


def spiked(entries, rng, source, target, shards_of, factor):
    owner, partner = [(jnp.arange(entries.shape[axis_at]) // (entries.shape[axis_at] // shards_of)).reshape([-1 if axis == axis_at else 1 for axis in range(entries.ndim)]) for axis_at in (source, target)]
    chosen = jax.random.permutation(rng, shards_of)[partner]
    strong = (owner == chosen) | (owner == (partner + shards_of // 2) % shards_of)
    return jnp.where(strong, factor * entries, entries)


def block_levels(stream_key, dims, cuts, smallest, high):
    loudness, own = 1.0, jax.random.fold_in(stream_key, 6)
    for axis_at, shards_of in cuts:
        steps = jnp.exp(jax.random.uniform(jax.random.fold_in(own, axis_at), (shards_of,), jnp.float32, smallest / len(cuts), high / len(cuts)))
        loudness = loudness * jnp.repeat(steps, dims[axis_at] // shards_of).reshape([-1 if axis == axis_at else 1 for axis in range(len(dims))])
    return loudness


def centred(own_key, extent, deviation, bound, cuts=(), kind=jnp.bfloat16):
    gain = block_levels(own_key, extent, cuts, -0.22, 0.18) if cuts else 1.0
    entries = jax.random.normal(own_key, extent, jnp.float32) * deviation * gain
    return jnp.minimum(jnp.maximum(entries, -bound), bound).astype(kind)


def noise_with(rng, extent, scale, most, cuts, heavy, held_as=jnp.bfloat16):
    array = scale * jax.random.normal(rng, extent, jnp.float32)
    if cuts:
        array = array * block_levels(rng, extent, cuts, -0.22, 0.18)
    return jnp.clip(spiked(array, jax.random.fold_in(rng, 3), *heavy), -most, most).astype(held_as)


def setup_inputs(seed: int = 0) -> dict:
    splits = jax.random.split(jax.random.key(seed), 5)
    return {
        "tokens_in": centred(splits[0], (TOKENS, BLOCK), 1.0, 6.0, ((0, 32), (1, 16))),
        "out_grads": noise_with(splits[1], (TOKENS, BLOCK), (BLOCK * TOKENS // 64) ** -0.5, 0.0078125, ((0, 32),), (0, 1, 32, 2.75)),
        "left_old": draw_left_old(jax.random.fold_in(splits[4], 71), 0),
        "right_old": draw_right_old(jax.random.fold_in(splits[4], 71), 0),
    }


ema_decay = 0.95


def reference(tokens_in, out_grads, left_old, right_old):
    grad = jnp.dot(tokens_in.T, out_grads, preferred_element_type=jnp.float32)
    grad_half = grad.astype(jnp.bfloat16)
    left_new = jnp.dot(grad_half, grad_half.T, preferred_element_type=jnp.float32)
    right_new = jnp.dot(grad_half.T, grad_half, preferred_element_type=jnp.float32)
    left_out = ema_decay * left_old + (1.0 - ema_decay) * left_new
    right_out = ema_decay * right_old + (1.0 - ema_decay) * right_new
    return left_out, right_out
```

```python
import jax
import jax.numpy as jnp
from jax import lax
from jax.experimental import pallas as pl
from jax.experimental.pallas import tpu as pltpu
from jax.sharding import PartitionSpec as P

MESH = pl.DeviceIdType.MESH
F32, BF16 = jnp.float32, jnp.bfloat16
decay = 0.95
NZ, NX, NODE = 16, 4, 16
TOK, BAND, WIDE, HALF, SUB = 1024, 256, 256, 128, 64


def dot(a, b):
    return lax.dot_general(a, b, (((1,), (0,)), ((), ())), preferred_element_type=F32)


def dot_t(a, b):
    return lax.dot_general(a, b, (((1,), (1,)), ((), ())), preferred_element_type=F32)


def group(g):
    return [0] if g == 0 else [8] if g == 8 else [g, NZ - g]


def kernel(
    tok, og, lold, rold, lout, rout,
    tokt, ogv, keep, ysend, yrecv, zsend, zrecv, ga, sib, at, rsend, rrecv, xt, bz, lacc, lrecv,
    og_sem, y_s, y_r, z_s, z_r, a_s, a_r, c_s, c_r, r_s, r_r, x_s, x_r, lz_s, lz_r, ly_s, lc_s, b_r, f_s, f_r,
):
    dp, node = lax.axis_index("dp"), lax.axis_index("node")
    z, yh = dp // 2, dp % 2
    yl, x, core = node // 8, (node // 2) % 4, node % 2
    y = yh * 2 + yl
    chip = yh * 8 + node // 2

    def at_z(k):
        return {"dp": ((z + k + NZ) % NZ) * 2 + yh, "node": node}

    def at_x(k):
        return {"dp": dp, "node": yl * 8 + ((x + k) % NX) * 2 + core}

    def at_y(k):
        yy = (y + k) % 4
        return {"dp": z * 2 + yy // 2, "node": (yy % 2) * 8 + x * 2 + core}

    partner = {"dp": z * 2 + 1 - yh, "node": node}
    sibling = {"dp": dp, "node": node + 1 - 2 * core}
    up, down = at_z(1), at_z(-1)

    def send(src, dst, ss, rs, to):
        return pltpu.make_async_remote_copy(
            src_ref=src, dst_ref=dst, send_sem=ss, recv_sem=rs, device_id=to, device_id_type=MESH
        )

    def og_copy(n):
        m = (n + 1) // 2
        t = 8 - m
        d = (z + jnp.where(n % 2 == 1, t, NZ - t)) % NZ
        return pltpu.make_async_copy(
            og.at[:, pl.ds(pl.multiple_of(d * WIDE, WIDE), WIDE)], ogv.at[n], og_sem.at[n]
        )

    barrier = pltpu.get_barrier_semaphore()
    for to in (up, down):
        pl.semaphore_signal(barrier, inc=1, device_id=to, device_id_type=MESH)

    def greet(k, carry):
        other = (node + k) % NODE
        pl.semaphore_signal(barrier, inc=1, device_id={"dp": z * 2 + 1 - yh, "node": other}, device_id_type=MESH)

        @pl.when(k > 0)
        def _():
            pl.semaphore_signal(barrier, inc=1, device_id={"dp": dp, "node": other}, device_id_type=MESH)

        return carry

    lax.fori_loop(0, NODE, greet, 0)

    def og_start(n, carry):
        og_copy(n).start()
        return carry

    lax.fori_loop(0, NZ, og_start, 0)

    for c in range(4):
        tokt[:, c * 256 : (c + 1) * 256] = tok[c * 256 : (c + 1) * 256, :].T
    pl.semaphore_wait(barrier, 2 + 31)

    def y_copy(n):
        return send(ysend.at[n], yrecv.at[n], y_s.at[n], y_r.at[n], partner)

    mine = pl.multiple_of(yh * HALF, HALF)
    theirs = pl.multiple_of((1 - yh) * HALF, HALF)

    def partial(n, carry):
        og_copy(n).wait()
        block = ogv.at[n]
        ysend[n] = dot(tokt[pl.ds(theirs, HALF), :], block[...]).astype(BF16)
        y_copy(n).start()
        keep[n] = dot(tokt[pl.ds(mine, HALF), :], block[...])
        return carry

    def z_copy(d, t, s):
        rows = pl.ds(s * SUB, SUB)
        return send(
            zsend.at[d, t - 1, rows], zrecv.at[d, t - 1, rows], z_s.at[d, t - 1, s], z_r.at[d, t - 1, s],
            up if d == 0 else down,
        )

    def z_has(d, t, s):
        return t < 8 or s == d

    def z_stage(t):
        for s in range(2):
            for d in range(2):
                if not z_has(d, t, s):
                    continue
                n = 0 if t == 8 else 2 * (8 - t) - 1 + d
                if t == 8 and d == 0 or t < 8 and s == 0:
                    y_copy(n).wait_recv()
                rows = pl.ds(s * SUB, SUB)
                value = keep[n, rows, :] + yrecv[n, rows, :].astype(F32)
                if t < 8 and z_has(d, t + 1, s):
                    z_copy(d, t + 1, s).wait_recv()
                    value = value + zrecv[d, t, rows, :]
                zsend[d, t - 1, rows, :] = value
                z_copy(d, t, s).start()

    def z_wait_send(t):
        for s in range(2):
            for d in range(2):
                if z_has(d, t, s):
                    z_copy(d, t, s).wait_send()

    lax.fori_loop(0, 9, partial, 0)
    z_stage(8)
    lax.fori_loop(9, 11, partial, 0)
    z_stage(7)
    lax.fori_loop(11, 13, partial, 0)
    z_stage(6)
    lax.fori_loop(13, 16, partial, 0)
    for t in range(5, 0, -1):
        z_stage(t)
    y_copy(15).wait_recv()
    for s in range(2):
        rows = pl.ds(s * SUB, SUB)
        value = keep[15, rows, :] + yrecv[15, rows, :].astype(F32)
        for d in range(2):
            z_copy(d, 1, s).wait_recv()
            value = value + zrecv[d, 0, rows, :]
        ga[0, rows, :] = value.astype(BF16)

    def a_has(d, k, s):
        return k < 8 or s == d

    def a_copy(d, k, s):
        rows = pl.ds(s * SUB, SUB)
        src, dst = ((NZ - k + 1) % NZ, NZ - k) if d == 0 else (k - 1, k)
        return send(
            ga.at[src, rows], ga.at[dst, rows], a_s.at[d, k - 1, s], a_r.at[d, k - 1, s], up if d == 0 else down
        )

    def c_copy(r):
        return send(ga.at[r], sib.at[r], c_s.at[r], c_r.at[r], sibling)

    def a_start(k):
        for s in range(2):
            for d in range(2):
                if k > 1 and a_has(d, k - 1, s):
                    a_copy(d, k - 1, s).wait_recv()
                if k < 9 and a_has(d, k, s):
                    a_copy(d, k, s).start()

    on_core = core == z % 2
    on_row = on_core & (yl == z // 8)

    def x_copy(k):
        slot = (NX - k) % NX
        return send(ga.at[0], xt.at[slot], x_s.at[k - 1], x_r.at[slot], at_x(k))

    def lz_plane(k):
        return yl * 8 + ((x + k) % NX) * 2 + core

    def lz_copy(k):
        plane = lz_plane(k)
        slot = (z - plane + NZ) % NZ
        return send(
            ga.at[0] if k == 0 else xt.at[k], bz.at[yh, slot], lz_s.at[k], b_r.at[yh, slot],
            {"dp": plane * 2 + yh, "node": node},
        )

    def bz_here(h, r):
        return send(bz.at[h, r], bz.at[h, r], f_s.at[0], b_r.at[h, r], partner)

    def ly_copy(k, r):
        return send(bz.at[yh, r], bz.at[yh, r], ly_s.at[r, k - 1], b_r.at[yh, r], at_y(k))

    def lc_copy(h, r):
        return send(bz.at[h, r], bz.at[h, r], lc_s.at[h, r], b_r.at[h, r], sibling)

    def left_z():
        for k in range(1, NX):
            x_copy((NX - k) % NX).wait_recv()
        for k in range(NX):
            away = lz_plane(k) != z

            @pl.when(away)
            def _():
                lz_copy(k).start()

            @pl.when(jnp.logical_not(away))
            def _():
                bz[yh, 0] = ga[0] if k == 0 else xt[k]

    def left_y(r):
        @pl.when(on_row)
        def _():
            if r != 0:
                bz_here(yh, r).wait_recv()
            for k in (1, 3, 2):
                ly_copy(k, r).start()

    def left_c(r):
        @pl.when(on_core)
        def _():
            for h in range(2):
                @pl.when(jnp.logical_not(on_row & (yh == h)))
                def _():
                    bz_here(h, r).wait_recv()

                lc_copy(h, r).start()

    def left_dot(r):
        @pl.when(jnp.logical_not(on_core))
        def _():
            for h in range(2):
                bz_here(h, r).wait_recv()

        for h in range(2):
            value = dot_t(ga[r], bz[h, r])
            lacc[h] = value if r == 0 else lacc[h] + value

    def r_copy(r):
        return send(
            rsend.at[r], rrecv.at[chip], r_s.at[r], r_r.at[chip], {"dp": z * 2 + core, "node": (z + r) % NZ}
        )

    def r_self(r):
        return (yh == core) & (node == (z + r) % NZ)

    def right_dot(r):
        c_copy(r).wait_recv()
        value = (dot(at[0], ga[r]) + dot(at[1], sib[r])).astype(BF16)

        @pl.when(r_self(r))
        def _():
            rrecv[chip] = value

        @pl.when(jnp.logical_not(r_self(r)))
        def _():
            rsend[r] = value
            r_copy(r).start()

    a_start(1)
    c_copy(0).start()
    for k in range(1, NX):
        x_copy(k).start()
    slab = pl.ds(pl.multiple_of(core * HALF, HALF), HALF)
    at[0] = ga[0, :, slab].astype(F32).T.astype(BF16)
    for t in range(8, 4, -1):
        z_wait_send(t)
    c_copy(0).wait_recv()
    at[1] = sib[0, :, slab].astype(F32).T.astype(BF16)

    y_groups = {2: [0], 3: [1, 2], 4: [3, 4], 5: [5, 6], 6: [7, 8]}
    for k in range(2, 10):
        step = k - 1
        a_start(k)
        for r in group(step):
            c_copy(r).start()
        if step == 1:
            left_z()
        if step == 1:
            value = (dot(at[0], ga[0]) + dot(at[1], sib[0])).astype(BF16)

            @pl.when(r_self(0))
            def _():
                rrecv[chip] = value

            @pl.when(jnp.logical_not(r_self(0)))
            def _():
                rsend[0] = value
                r_copy(0).start()
        else:
            for r in group(step - 1):
                right_dot(r)
        for g in y_groups.get(step, []):
            for r in group(g):
                left_y(r)
        for g in y_groups.get(step - 1, []):
            for r in group(g):
                left_c(r)
        for g in y_groups.get(step - 2, []):
            for r in group(g):
                left_dot(r)
    right_dot(8)

    def f_copy():
        return send(lacc.at[1 - yh], lrecv, f_s.at[0], f_r.at[0], partner)

    f_copy().start()
    lout[pl.ds(mine, HALF), :] = decay * lold[pl.ds(mine, HALF), :] + (1.0 - decay) * lacc[yh]

    def r_here(i):
        return send(rrecv.at[i], rrecv.at[i], r_s.at[0], r_r.at[i], partner)

    total = None
    for i in range(NZ):
        @pl.when(jnp.logical_not((core == yh) & (chip == i)))
        def _():
            r_here(i).wait_recv()

        piece = rrecv[i].astype(F32)
        total = piece if total is None else total + piece
    rout[...] = decay * rold[...] + (1.0 - decay) * total.T
    f_copy().wait_recv()
    lout[pl.ds(theirs, HALF), :] = decay * lold[pl.ds(theirs, HALF), :] + (1.0 - decay) * lrecv[...]
    f_copy().wait_send()

    for t in range(4, 0, -1):
        z_wait_send(t)
    for k in range(1, 9):
        for s in range(2):
            for d in range(2):
                if a_has(d, k, s):
                    a_copy(d, k, s).wait_send()
    for k in range(1, NX):
        x_copy(k).wait_send()
    for k in range(NX):
        @pl.when(lz_plane(k) != z)
        def _():
            lz_copy(k).wait_send()

    def drain(n, carry):
        y_copy(n).wait_send()
        return carry

    lax.fori_loop(0, NZ, drain, 0)
    for r in range(NZ):
        c_copy(r).wait_send()

        @pl.when(jnp.logical_not(r_self(r)))
        def _():
            r_copy(r).wait_send()

        @pl.when(on_row)
        def _():
            for k in (1, 3, 2):
                ly_copy(k, r).wait_send()

        @pl.when(on_core)
        def _():
            for h in range(2):
                lc_copy(h, r).wait_send()


def shards(tokens_in, out_grads, left_old, right_old):
    dma = pltpu.SemaphoreType.DMA
    vmem = pl.BlockSpec(memory_space=pltpu.VMEM)
    return pl.pallas_call(
        kernel,
        out_shape=(jax.ShapeDtypeStruct((BAND, HALF), F32),) * 2,
        in_specs=[vmem, pl.BlockSpec(memory_space=pl.ANY), vmem, vmem],
        out_specs=(vmem, vmem),
        scratch_shapes=[
            pltpu.VMEM((BAND, TOK), BF16),
            pltpu.VMEM((NZ, TOK, WIDE), BF16),
            pltpu.VMEM((NZ, HALF, WIDE), F32),
            pltpu.VMEM((NZ, HALF, WIDE), BF16),
            pltpu.VMEM((NZ, HALF, WIDE), BF16),
            pltpu.VMEM((2, 8, HALF, WIDE), F32),
            pltpu.VMEM((2, 8, HALF, WIDE), F32),
            pltpu.VMEM((NZ, HALF, WIDE), BF16),
            pltpu.VMEM((NZ, HALF, WIDE), BF16),
            pltpu.VMEM((2, HALF, HALF), BF16),
            pltpu.VMEM((NZ, HALF, WIDE), BF16),
            pltpu.VMEM((NZ, HALF, WIDE), BF16),
            pltpu.VMEM((NX, HALF, WIDE), BF16),
            pltpu.VMEM((2, NZ, HALF, WIDE), BF16),
            pltpu.VMEM((2, HALF, HALF), F32),
            pltpu.VMEM((HALF, HALF), F32),
            dma((NZ,)), dma((NZ,)), dma((NZ,)),
            dma((2, 8, 2)), dma((2, 8, 2)),
            dma((2, 8, 2)), dma((2, 8, 2)),
            dma((NZ,)), dma((NZ,)),
            dma((NZ,)), dma((NZ,)),
            dma((3,)), dma((4,)),
            dma((4,)), dma((1,)),
            dma((NZ, 3)), dma((2, NZ)), dma((2, NZ)),
            dma((1,)), dma((1,)),
        ],
        compiler_params=pltpu.CompilerParams(
            collective_id=0, has_side_effects=True, vmem_limit_bytes=48 * 2**20
        ),
        cost_estimate=pl.CostEstimate(flops=2 * TOK * BAND * 4096, bytes_accessed=TOK * 4096 * 2, transcendentals=0),
    )(tokens_in, out_grads, left_old, right_old)


def solution(mesh):
    return jax.shard_map(
        shards,
        mesh=mesh,
        in_specs=(P("dp", "node"), P("dp", None), P("node", "dp"), P("node", "dp")),
        out_specs=(P("node", "dp"), P("node", "dp")),
        check_vma=False,
    )
```

```python
import jax
import jax.numpy as jnp
from jax import lax
from jax.experimental import pallas as pl
from jax.experimental.pallas import tpu as pltpu
from jax.sharding import PartitionSpec as P

MESH = pl.DeviceIdType.MESH
F32, BF16 = jnp.float32, jnp.bfloat16
decay = 0.95
NZ, NODE = 16, 16
TOK, BAND, WIDE, HALF, SUB = 1024, 256, 256, 128, 64
PARTS = 4
PART = HALF // PARTS


def dot(a, b):
    return lax.dot_general(a, b, (((1,), (0,)), ((), ())), preferred_element_type=F32)


def dot_t(a, b):
    return lax.dot_general(a, b, (((1,), (1,)), ((), ())), preferred_element_type=F32)


def group(g):
    return [0] if g == 0 else [8] if g == 8 else [g, NZ - g]


def kernel(
    tok_in, og, lold_in, rold_in, lout, rout,
    tok, lold, rold, tokt, ogv, keep, ysend, yrecv, zsend, zrecv, ga, at, rsend, rrecv, bz, lacc, lrecv,
    in_sem, og_sem, y_s, y_r, z_s, z_r, a_s, a_r, c_s, c_r, r_s, r_r, t_s, b_s, b_r, f_s, f_r,
):
    dp, node = lax.axis_index("dp"), lax.axis_index("node")
    z, yh = dp // 2, dp % 2
    core = node % 2
    chip = yh * 8 + node // 2

    def at_z(k):
        return {"dp": ((z + k + NZ) % NZ) * 2 + yh, "node": node}

    partner = {"dp": z * 2 + 1 - yh, "node": node}
    sibling = {"dp": dp, "node": node + 1 - 2 * core}
    up, down = at_z(1), at_z(-1)

    def send(src, dst, ss, rs, to):
        return pltpu.make_async_remote_copy(
            src_ref=src, dst_ref=dst, send_sem=ss, recv_sem=rs, device_id=to, device_id_type=MESH
        )

    def og_copy(n):
        m = (n + 1) // 2
        t = 8 - m
        d = (z + jnp.where(n % 2 == 1, t, NZ - t)) % NZ
        return pltpu.make_async_copy(
            og.at[:, pl.ds(pl.multiple_of(d * WIDE, WIDE), WIDE)], ogv.at[n], og_sem.at[n]
        )

    def og_start(n, carry):
        og_copy(n).start()
        return carry

    ins = [
        pltpu.make_async_copy(src, dst, in_sem.at[i])
        for i, (src, dst) in enumerate(((tok_in, tok), (lold_in, lold), (rold_in, rold)))
    ]
    ins[0].start()
    barrier = pltpu.get_barrier_semaphore()
    for to in (up, down):
        pl.semaphore_signal(barrier, inc=1, device_id=to, device_id_type=MESH)

    def greet(k, carry):
        other = (node + k) % NODE
        pl.semaphore_signal(barrier, inc=1, device_id={"dp": z * 2 + 1 - yh, "node": other}, device_id_type=MESH)

        @pl.when(k > 0)
        def _():
            pl.semaphore_signal(barrier, inc=1, device_id={"dp": dp, "node": other}, device_id_type=MESH)

        return carry

    lax.fori_loop(0, NODE, greet, 0)
    moves = jnp.logical_not((node == z) & (chip == z) & (core == yh))

    @pl.when(moves)
    def _():
        pl.semaphore_signal(
            barrier, inc=1, device_id={"dp": chip * 2 + core, "node": z}, device_id_type=MESH
        )

    lax.fori_loop(0, NZ, og_start, 0)
    ins[1].start()
    ins[2].start()
    ins[0].wait()
    for c in range(4):
        tokt[:, c * 256 : (c + 1) * 256] = tok[c * 256 : (c + 1) * 256, :].T
    pl.semaphore_wait(barrier, jnp.where(moves, 34, 33))

    def y_copy(n):
        return send(ysend.at[n], yrecv.at[n], y_s.at[n], y_r.at[n], partner)

    mine = pl.multiple_of(yh * HALF, HALF)
    theirs = pl.multiple_of((1 - yh) * HALF, HALF)

    def partial(n, carry):
        og_copy(n).wait()
        block = ogv.at[n]
        ysend[n] = dot(tokt[pl.ds(theirs, HALF), :], block[...]).astype(BF16)
        y_copy(n).start()
        keep[n] = dot(tokt[pl.ds(mine, HALF), :], block[...])
        return carry

    def z_copy(d, t, s):
        rows = pl.ds(s * PART, PART)
        return send(
            zsend.at[d, t - 1, rows], zrecv.at[d, t - 1, rows], z_s.at[d, t - 1, s], z_r.at[d, t - 1, s],
            up if d == 0 else down,
        )

    def z_has(d, t, s):
        return t < 8 or s // (PARTS // 2) == d

    def z_stage(t):
        for s in range(PARTS):
            for d in range(2):
                if not z_has(d, t, s):
                    continue
                n = 0 if t == 8 else 2 * (8 - t) - 1 + d
                if s == 0:
                    y_copy(n).wait_recv()
                rows = pl.ds(s * PART, PART)
                value = keep[n, rows, :] + yrecv[n, rows, :].astype(F32)
                if t < 8 and z_has(d, t + 1, s):
                    z_copy(d, t + 1, s).wait_recv()
                    value = value + zrecv[d, t, rows, :]
                zsend[d, t - 1, rows, :] = value
                z_copy(d, t, s).start()

    def z_wait_send(t):
        for s in range(PARTS):
            for d in range(2):
                if z_has(d, t, s):
                    z_copy(d, t, s).wait_send()

    lax.fori_loop(0, 7, partial, 0)
    z_stage(8)
    lax.fori_loop(7, 10, partial, 0)
    z_stage(7)
    lax.fori_loop(10, 13, partial, 0)
    z_stage(6)
    lax.fori_loop(13, 16, partial, 0)
    for t in range(5, 0, -1):
        z_stage(t)
    y_copy(15).wait_recv()
    for s in range(PARTS):
        rows = pl.ds(s * PART, PART)
        value = keep[15, rows, :] + yrecv[15, rows, :].astype(F32)
        for d in range(2):
            z_copy(d, 1, s).wait_recv()
            value = value + zrecv[d, 0, rows, :]
        ga[0, rows, :] = value.astype(BF16)

    def a_has(d, k, s):
        return k < 8 or s == d

    def a_copy(d, k, s):
        rows = pl.ds(s * SUB, SUB)
        src, dst = ((NZ - k + 1) % NZ, NZ - k) if d == 0 else (k - 1, k)
        return send(
            ga.at[src, rows], ga.at[dst, rows], a_s.at[d, k - 1, s], a_r.at[d, k - 1, s], up if d == 0 else down
        )

    def c_copy(r):
        return send(ga.at[r, pl.ds(0, HALF)], ga.at[r, pl.ds(HALF, HALF)], c_s.at[r], c_r.at[r], sibling)

    def a_start(k):
        for s in range(2):
            for d in range(2):
                if k > 1 and a_has(d, k - 1, s):
                    a_copy(d, k - 1, s).wait_recv()
                if k < 9 and a_has(d, k, s):
                    a_copy(d, k, s).start()

    own = (chip - z + NZ) % NZ
    stays = (node == z) & (chip == z) & (core == yh)

    def t_copy():
        return send(
            ga.at[0, pl.ds(0, HALF)], bz.at[(z - node + NZ) % NZ], t_s.at[0], b_r.at[(z - node + NZ) % NZ],
            {"dp": node * 2 + z // 8, "node": (z % 8) * 2 + yh},
        )

    def b_here(r):
        return send(bz.at[r], bz.at[r], t_s.at[0], b_r.at[r], partner)

    def b_copy(k):
        to = (chip + k) % NZ
        return send(
            bz.at[own], bz.at[own], b_s.at[k - 1], b_r.at[own], {"dp": z * 2 + to // 8, "node": (to % 8) * 2 + core}
        )

    def left_spread(low, high):
        far = jnp.minimum(own, NZ - own)

        @pl.when((far >= low) & (far <= high))
        def _():
            @pl.when(jnp.logical_not(stays))
            def _():
                b_here(own).wait_recv()

            def go(k, carry):
                b_copy(k).start()
                return carry

            lax.fori_loop(1, NZ, go, 0)

    def left_dot(groups):
        tiles = [r for g in groups for r in group(g)]
        for r in tiles:
            @pl.when(own != r)
            def _():
                b_here(r).wait_recv()

        value = lacc[...] if tiles[0] != 0 else None
        for r in tiles:
            term = dot_t(ga[r], bz[r])
            value = term if value is None else value + term
        lacc[...] = value

    def r_copy(r):
        return send(
            rsend.at[r], rrecv.at[chip], r_s.at[r], r_r.at[chip], {"dp": z * 2 + core, "node": (z + r) % NZ}
        )

    def r_self(r):
        return (yh == core) & (node == (z + r) % NZ)

    def right_dot(r):
        value = dot(at[...], ga[r]).astype(BF16)

        @pl.when(r_self(r))
        def _():
            rrecv[chip] = value

        @pl.when(jnp.logical_not(r_self(r)))
        def _():
            rsend[r] = value
            r_copy(r).start()

    a_start(1)
    c_copy(0).start()

    @pl.when(stays)
    def _():
        bz[0] = ga[0, :HALF, :]

    @pl.when(jnp.logical_not(stays))
    def _():
        t_copy().start()

    slab = pl.ds(pl.multiple_of(core * HALF, HALF), HALF)
    c_copy(0).wait_recv()
    at[...] = ga[0, :, slab].astype(F32).T.astype(BF16)
    def drain(n, carry):
        y_copy(n).wait_send()
        return carry

    right_at = {5: (0, 1, 2), 6: (3, 4, 5), 7: (6, 7), 8: (8,)}
    for step in range(1, 9):
        a_start(step + 1)
        for r in group(step):
            c_copy(r).start()
        if step == 1:
            z_wait_send(8)
            z_wait_send(7)
            lax.fori_loop(0, NZ, drain, 0)
        if step == 2:
            left_spread(0, 2)
        if step == 3:
            left_spread(3, 5)
        if step == 4:
            left_spread(6, 8)
        for r in group(step):
            c_copy(r).wait_recv()
        for g in right_at.get(step, ()):
            for r in group(g):
                right_dot(r)
        if step == 7:
            left_dot((0, 1, 2))
        if step in (1, 2, 3):
            z_wait_send(8 - 2 * step)
            z_wait_send(7 - 2 * step)
    left_dot((3, 4, 5))
    left_dot((6, 7, 8))

    ins[1].wait()
    ins[2].wait()

    def f_copy(j):
        return send(
            lacc.at[pl.ds(j * HALF, HALF)], lrecv.at[yh], f_s.at[j], f_r.at[yh],
            {"dp": z * 2 + core, "node": node if j == 0 else node + 1 - 2 * core},
        )

    def f_here(h):
        return send(lrecv.at[h], lrecv.at[h], f_s.at[0], f_r.at[h], partner)

    f_copy(1).start()

    @pl.when(yh == core)
    def _():
        lrecv[yh] = lacc[:HALF, :]

    @pl.when(yh != core)
    def _():
        f_copy(0).start()

    def r_here(i):
        return send(rrecv.at[i], rrecv.at[i], r_s.at[0], r_r.at[i], partner)

    total = None
    for i in range(NZ):
        @pl.when(jnp.logical_not((core == yh) & (chip == i)))
        def _():
            r_here(i).wait_recv()

        piece = rrecv[i].astype(F32)
        total = piece if total is None else total + piece
    rout[...] = decay * rold[...] + (1.0 - decay) * total.T
    for h in range(2):
        @pl.when(jnp.logical_not((core == yh) & (yh == h)))
        def _():
            f_here(h).wait_recv()

        rows = slice(h * HALF, (h + 1) * HALF)
        lout[rows, :] = decay * lold[rows, :] + (1.0 - decay) * lrecv[h]

    f_copy(1).wait_send()

    @pl.when(yh != core)
    def _():
        f_copy(0).wait_send()

    for k in range(1, 9):
        for s in range(2):
            for d in range(2):
                if a_has(d, k, s):
                    a_copy(d, k, s).wait_send()

    @pl.when(jnp.logical_not(stays))
    def _():
        t_copy().wait_send()

    def b_drain(k, carry):
        b_copy(k).wait_send()
        return carry

    lax.fori_loop(1, NZ, b_drain, 0)
    for r in range(NZ):
        c_copy(r).wait_send()

        @pl.when(jnp.logical_not(r_self(r)))
        def _():
            r_copy(r).wait_send()


def shards(tokens_in, out_grads, left_old, right_old):
    dma = pltpu.SemaphoreType.DMA
    vmem = pl.BlockSpec(memory_space=pltpu.VMEM)
    return pl.pallas_call(
        kernel,
        out_shape=(jax.ShapeDtypeStruct((BAND, HALF), F32),) * 2,
        in_specs=[pl.BlockSpec(memory_space=pl.ANY)] * 4,
        out_specs=(vmem, vmem),
        scratch_shapes=[
            pltpu.VMEM((TOK, BAND), BF16),
            pltpu.VMEM((BAND, HALF), F32),
            pltpu.VMEM((BAND, HALF), F32),
            pltpu.VMEM((BAND, TOK), BF16),
            pltpu.VMEM((NZ, TOK, WIDE), BF16),
            pltpu.VMEM((NZ, HALF, WIDE), F32),
            pltpu.VMEM((NZ, HALF, WIDE), BF16),
            pltpu.VMEM((NZ, HALF, WIDE), BF16),
            pltpu.VMEM((2, 8, HALF, WIDE), F32),
            pltpu.VMEM((2, 8, HALF, WIDE), F32),
            pltpu.VMEM((NZ, BAND, WIDE), BF16),
            pltpu.VMEM((HALF, BAND), BF16),
            pltpu.VMEM((NZ, HALF, WIDE), BF16),
            pltpu.VMEM((NZ, HALF, WIDE), BF16),
            pltpu.VMEM((NZ, HALF, WIDE), BF16),
            pltpu.VMEM((BAND, HALF), F32),
            pltpu.VMEM((2, HALF, HALF), F32),
            dma((3,)), dma((NZ,)), dma((NZ,)), dma((NZ,)),
            dma((2, 8, PARTS)), dma((2, 8, PARTS)),
            dma((2, 8, 2)), dma((2, 8, 2)),
            dma((NZ,)), dma((NZ,)),
            dma((NZ,)), dma((NZ,)),
            dma((1,)), dma((NZ - 1,)), dma((NZ,)),
            dma((2,)), dma((2,)),
        ],
        compiler_params=pltpu.CompilerParams(
            collective_id=0, has_side_effects=True, vmem_limit_bytes=60 * 2**20
        ),
        cost_estimate=pl.CostEstimate(flops=2 * TOK * BAND * 4096, bytes_accessed=TOK * 4096 * 2, transcendentals=0),
    )(tokens_in, out_grads, left_old, right_old)


def solution(mesh):
    return jax.shard_map(
        shards,
        mesh=mesh,
        in_specs=(P("dp", "node"), P("dp", None), P("node", "dp"), P("node", "dp")),
        out_specs=(P("node", "dp"), P("node", "dp")),
        check_vma=False,
    )
```

```python
import jax
import jax.numpy as jnp
from jax import lax
from jax.experimental import pallas as pl
from jax.experimental.pallas import tpu as pltpu
from jax.sharding import PartitionSpec as P

MESH = pl.DeviceIdType.MESH
F32, BF16 = jnp.float32, jnp.bfloat16
decay = 0.95
NZ, NODE = 16, 16
TOK, BAND, WIDE, HALF, SUB = 1024, 256, 256, 128, 64
PARTS = 4
PART = HALF // PARTS


def dot(a, b):
    return lax.dot_general(a, b, (((1,), (0,)), ((), ())), preferred_element_type=F32)


def dot_t(a, b):
    return lax.dot_general(a, b, (((1,), (1,)), ((), ())), preferred_element_type=F32)


def group(g):
    return [0] if g == 0 else [8] if g == 8 else [g, NZ - g]


def kernel(
    tok_in, og, lout, rout,
    tok, tokt, ogv, keep, ysend, yrecv, zsend, zrecv, ga, at, rsend, rrecv, bz, lacc, lrecv,
    in_sem, og_sem, y_s, y_r, z_s, z_r, a_s, a_r, c_s, c_r, r_s, r_r, t_s, b_s, b_r, f_s, f_r,
):
    dp, node = lax.axis_index("dp"), lax.axis_index("node")
    z, yh = dp // 2, dp % 2
    core = node % 2
    chip = yh * 8 + node // 2

    def at_z(k):
        return {"dp": ((z + k + NZ) % NZ) * 2 + yh, "node": node}

    partner = {"dp": z * 2 + 1 - yh, "node": node}
    sibling = {"dp": dp, "node": node + 1 - 2 * core}
    up, down = at_z(1), at_z(-1)

    def send(src, dst, ss, rs, to):
        return pltpu.make_async_remote_copy(
            src_ref=src, dst_ref=dst, send_sem=ss, recv_sem=rs, device_id=to, device_id_type=MESH
        )

    def og_copy(n):
        m = (n + 1) // 2
        t = 8 - m
        d = (z + jnp.where(n % 2 == 1, t, NZ - t)) % NZ
        return pltpu.make_async_copy(
            og.at[:, pl.ds(pl.multiple_of(d * WIDE, WIDE), WIDE)], ogv.at[n], og_sem.at[n]
        )

    def og_start(n, carry):
        og_copy(n).start()
        return carry

    tok_copy = pltpu.make_async_copy(tok_in, tok, in_sem.at[0])
    tok_copy.start()
    for n in range(3):
        og_copy(n).start()
    barrier = pltpu.get_barrier_semaphore()
    for to in (up, down):
        pl.semaphore_signal(barrier, inc=1, device_id=to, device_id_type=MESH)

    def greet(k, carry):
        other = (node + k) % NODE
        pl.semaphore_signal(barrier, inc=1, device_id={"dp": z * 2 + 1 - yh, "node": other}, device_id_type=MESH)

        @pl.when(k > 0)
        def _():
            pl.semaphore_signal(barrier, inc=1, device_id={"dp": dp, "node": other}, device_id_type=MESH)

        return carry

    lax.fori_loop(0, NODE, greet, 0)
    moves = jnp.logical_not((node == z) & (chip == z) & (core == yh))

    @pl.when(moves)
    def _():
        pl.semaphore_signal(
            barrier, inc=1, device_id={"dp": chip * 2 + core, "node": z}, device_id_type=MESH
        )

    lax.fori_loop(3, NZ, og_start, 0)
    tok_copy.wait()
    for c in range(4):
        tokt[:, c * 256 : (c + 1) * 256] = tok[c * 256 : (c + 1) * 256, :].T
    pl.semaphore_wait(barrier, jnp.where(moves, 34, 33))

    def y_copy(n):
        return send(ysend.at[n], yrecv.at[n], y_s.at[n], y_r.at[n], partner)

    mine = pl.multiple_of(yh * HALF, HALF)
    theirs = pl.multiple_of((1 - yh) * HALF, HALF)

    def partial(n, carry):
        og_copy(n).wait()
        block = ogv.at[n]
        ysend[n] = dot(tokt[pl.ds(theirs, HALF), :], block[...]).astype(BF16)
        y_copy(n).start()
        keep[n] = dot(tokt[pl.ds(mine, HALF), :], block[...])
        return carry

    def z_copy(d, t, s):
        rows = pl.ds(s * PART, PART)
        return send(
            zsend.at[d, t - 1, rows], zrecv.at[d, t - 1, rows], z_s.at[d, t - 1, s], z_r.at[d, t - 1, s],
            up if d == 0 else down,
        )

    def z_has(d, t, s):
        return t < 8 or s // (PARTS // 2) == d

    def z_stage(t):
        for s in range(PARTS):
            for d in range(2):
                if not z_has(d, t, s):
                    continue
                n = 0 if t == 8 else 2 * (8 - t) - 1 + d
                if s == 0:
                    y_copy(n).wait_recv()
                rows = pl.ds(s * PART, PART)
                value = keep[n, rows, :] + yrecv[n, rows, :].astype(F32)
                if t < 8 and z_has(d, t + 1, s):
                    z_copy(d, t + 1, s).wait_recv()
                    value = value + zrecv[d, t, rows, :]
                zsend[d, t - 1, rows, :] = value
                z_copy(d, t, s).start()

    def z_wait_send(t):
        for s in range(PARTS):
            for d in range(2):
                if z_has(d, t, s):
                    z_copy(d, t, s).wait_send()

    lax.fori_loop(0, 7, partial, 0)
    z_stage(8)
    lax.fori_loop(7, 10, partial, 0)
    z_stage(7)
    lax.fori_loop(10, 13, partial, 0)
    z_stage(6)
    lax.fori_loop(13, 16, partial, 0)
    for t in range(5, 0, -1):
        z_stage(t)
    y_copy(15).wait_recv()
    for s in range(PARTS):
        rows = pl.ds(s * PART, PART)
        value = keep[15, rows, :] + yrecv[15, rows, :].astype(F32)
        for d in range(2):
            z_copy(d, 1, s).wait_recv()
            value = value + zrecv[d, 0, rows, :]
        ga[0, rows, :] = value.astype(BF16)

    def a_has(d, k, s):
        return k < 8 or s == d

    def a_copy(d, k, s):
        rows = pl.ds(s * SUB, SUB)
        src, dst = ((NZ - k + 1) % NZ, NZ - k) if d == 0 else (k - 1, k)
        return send(
            ga.at[src, rows], ga.at[dst, rows], a_s.at[d, k - 1, s], a_r.at[d, k - 1, s], up if d == 0 else down
        )

    def c_copy(r):
        return send(ga.at[r, pl.ds(0, HALF)], ga.at[r, pl.ds(HALF, HALF)], c_s.at[r], c_r.at[r], sibling)

    def a_start(k):
        for s in range(2):
            for d in range(2):
                if k > 1 and a_has(d, k - 1, s):
                    a_copy(d, k - 1, s).wait_recv()
                if k < 9 and a_has(d, k, s):
                    a_copy(d, k, s).start()

    own = (chip - z + NZ) % NZ
    stays = (node == z) & (chip == z) & (core == yh)

    def t_copy():
        return send(
            ga.at[0, pl.ds(0, HALF)], bz.at[(z - node + NZ) % NZ], t_s.at[0], b_r.at[(z - node + NZ) % NZ],
            {"dp": node * 2 + z // 8, "node": (z % 8) * 2 + yh},
        )

    def b_here(r):
        return send(bz.at[r], bz.at[r], t_s.at[0], b_r.at[r], partner)

    def b_copy(k):
        to = (chip + k) % NZ
        return send(
            bz.at[own], bz.at[own], b_s.at[k - 1], b_r.at[own], {"dp": z * 2 + to // 8, "node": (to % 8) * 2 + core}
        )

    def left_spread(low, high):
        far = jnp.minimum(own, NZ - own)

        @pl.when((far >= low) & (far <= high))
        def _():
            @pl.when(jnp.logical_not(stays))
            def _():
                b_here(own).wait_recv()

            def go(k, carry):
                b_copy(k).start()
                return carry

            lax.fori_loop(1, NZ, go, 0)

    def left_dot(groups):
        tiles = [r for g in groups for r in group(g)]
        for r in tiles:
            @pl.when(own != r)
            def _():
                b_here(r).wait_recv()

        value = lacc[...] if tiles[0] != 0 else None
        for r in tiles:
            term = dot_t(ga[r], bz[r])
            value = term if value is None else value + term
        lacc[...] = value

    def r_copy(r):
        return send(
            rsend.at[r], rrecv.at[chip], r_s.at[r], r_r.at[chip], {"dp": z * 2 + core, "node": (z + r) % NZ}
        )

    def r_self(r):
        return (yh == core) & (node == (z + r) % NZ)

    def right_dot(r):
        value = dot(at[...], ga[r]).astype(BF16)

        @pl.when(r_self(r))
        def _():
            rrecv[chip] = value

        @pl.when(jnp.logical_not(r_self(r)))
        def _():
            rsend[r] = value
            r_copy(r).start()

    a_start(1)
    c_copy(0).start()

    @pl.when(stays)
    def _():
        bz[0] = ga[0, :HALF, :]

    @pl.when(jnp.logical_not(stays))
    def _():
        t_copy().start()

    slab = pl.ds(pl.multiple_of(core * HALF, HALF), HALF)
    c_copy(0).wait_recv()
    at[...] = ga[0, :, slab].astype(F32).T.astype(BF16)
    def drain(n, carry):
        y_copy(n).wait_send()
        return carry

    right_at = {5: (0, 1, 2), 6: (3, 4, 5), 7: (6, 7), 8: (8,)}
    for step in range(1, 9):
        a_start(step + 1)
        for r in group(step):
            c_copy(r).start()
        if step == 1:
            z_wait_send(8)
            z_wait_send(7)
            lax.fori_loop(0, NZ, drain, 0)
        if step == 2:
            left_spread(0, 2)
        if step == 3:
            left_spread(3, 5)
        if step == 4:
            left_spread(6, 8)
        for r in group(step):
            c_copy(r).wait_recv()
        for g in right_at.get(step, ()):
            for r in group(g):
                right_dot(r)
        if step == 7:
            left_dot((0, 1, 2))
        if step in (1, 2, 3):
            z_wait_send(8 - 2 * step)
            z_wait_send(7 - 2 * step)
    left_dot((3, 4, 5))
    left_dot((6, 7, 8))

    def f_copy(j):
        return send(
            lacc.at[pl.ds(j * HALF, HALF)], lrecv.at[yh], f_s.at[j], f_r.at[yh],
            {"dp": z * 2 + core, "node": node if j == 0 else node + 1 - 2 * core},
        )

    def f_here(h):
        return send(lrecv.at[h], lrecv.at[h], f_s.at[0], f_r.at[h], partner)

    f_copy(1).start()

    @pl.when(yh == core)
    def _():
        lrecv[yh] = lacc[:HALF, :]

    @pl.when(yh != core)
    def _():
        f_copy(0).start()

    for k in range(1, 9):
        for s in range(2):
            for d in range(2):
                if a_has(d, k, s):
                    a_copy(d, k, s).wait_send()

    @pl.when(jnp.logical_not(stays))
    def _():
        t_copy().wait_send()

    def b_drain(k, carry):
        b_copy(k).wait_send()
        return carry

    lax.fori_loop(1, NZ, b_drain, 0)
    for r in range(NZ):
        c_copy(r).wait_send()

    def r_here(i):
        return send(rrecv.at[i], rrecv.at[i], r_s.at[0], r_r.at[i], partner)

    total = None
    for i in range(NZ):
        @pl.when(jnp.logical_not((core == yh) & (chip == i)))
        def _():
            r_here(i).wait_recv()

        piece = rrecv[i].astype(F32)
        total = piece if total is None else total + piece
    rout[...] = total.T
    for h in range(2):
        @pl.when(jnp.logical_not((core == yh) & (yh == h)))
        def _():
            f_here(h).wait_recv()

        rows = slice(h * HALF, (h + 1) * HALF)
        lout[rows, :] = lrecv[h]

    f_copy(1).wait_send()

    @pl.when(yh != core)
    def _():
        f_copy(0).wait_send()

    for r in range(NZ):
        @pl.when(jnp.logical_not(r_self(r)))
        def _():
            r_copy(r).wait_send()


def shards(tokens_in, out_grads, left_old, right_old):
    dma = pltpu.SemaphoreType.DMA
    vmem = pl.BlockSpec(memory_space=pltpu.VMEM)
    left_new, right_new = pl.pallas_call(
        kernel,
        out_shape=(jax.ShapeDtypeStruct((BAND, HALF), F32),) * 2,
        in_specs=[pl.BlockSpec(memory_space=pl.ANY)] * 2,
        out_specs=(vmem, vmem),
        scratch_shapes=[
            pltpu.VMEM((TOK, BAND), BF16),
            pltpu.VMEM((BAND, TOK), BF16),
            pltpu.VMEM((NZ, TOK, WIDE), BF16),
            pltpu.VMEM((NZ, HALF, WIDE), F32),
            pltpu.VMEM((NZ, HALF, WIDE), BF16),
            pltpu.VMEM((NZ, HALF, WIDE), BF16),
            pltpu.VMEM((2, 8, HALF, WIDE), F32),
            pltpu.VMEM((2, 8, HALF, WIDE), F32),
            pltpu.VMEM((NZ, BAND, WIDE), BF16),
            pltpu.VMEM((HALF, BAND), BF16),
            pltpu.VMEM((NZ, HALF, WIDE), BF16),
            pltpu.VMEM((NZ, HALF, WIDE), BF16),
            pltpu.VMEM((NZ, HALF, WIDE), BF16),
            pltpu.VMEM((BAND, HALF), F32),
            pltpu.VMEM((2, HALF, HALF), F32),
            dma((1,)), dma((NZ,)), dma((NZ,)), dma((NZ,)),
            dma((2, 8, PARTS)), dma((2, 8, PARTS)),
            dma((2, 8, 2)), dma((2, 8, 2)),
            dma((NZ,)), dma((NZ,)),
            dma((NZ,)), dma((NZ,)),
            dma((1,)), dma((NZ - 1,)), dma((NZ,)),
            dma((2,)), dma((2,)),
        ],
        compiler_params=pltpu.CompilerParams(
            collective_id=0, has_side_effects=True, vmem_limit_bytes=60 * 2**20
        ),
        cost_estimate=pl.CostEstimate(flops=2 * TOK * BAND * 4096, bytes_accessed=TOK * 4096 * 2, transcendentals=0),
    )(tokens_in, out_grads)
    left_out = decay * left_old + (1.0 - decay) * left_new
    right_out = decay * right_old + (1.0 - decay) * right_new
    return left_out, right_out


def solution(mesh):
    return jax.shard_map(
        shards,
        mesh=mesh,
        in_specs=(P("dp", "node"), P("dp", None), P("node", "dp"), P("node", "dp")),
        out_specs=(P("node", "dp"), P("node", "dp")),
        check_vma=False,
    )
```

```python
import jax
import jax.numpy as jnp
from jax import lax
from jax.experimental import pallas as pl
from jax.experimental.pallas import tpu as pltpu
from jax.sharding import PartitionSpec as P

MESH = pl.DeviceIdType.MESH
F32, BF16 = jnp.float32, jnp.bfloat16
decay = 0.95
NZ, NODE = 16, 16
TOK, BAND, WIDE, HALF, SUB = 1024, 256, 256, 128, 64
PARTS = 4
PART = HALF // PARTS


def dot(a, b):
    return lax.dot_general(a, b, (((1,), (0,)), ((), ())), preferred_element_type=F32)


def dot_t(a, b):
    return lax.dot_general(a, b, (((1,), (1,)), ((), ())), preferred_element_type=F32)


def group(g):
    return [0] if g == 0 else [8] if g == 8 else [g, NZ - g]


def kernel(
    tok_in, og, lout, rout,
    tok, tokt, ogv, keep, ysend, yrecv, zsend, zrecv, ga, at, rsend, rrecv, bz, lacc, lrecv,
    in_sem, og_sem, y_s, y_r, z_s, z_r, a_s, a_r, c_s, c_r, r_s, r_r, t_s, b_s, b_r, f_s, f_r,
):
    dp, node = lax.axis_index("dp"), lax.axis_index("node")
    z, yh = dp // 2, dp % 2
    core = node % 2
    chip = yh * 8 + node // 2

    def at_z(k):
        return {"dp": ((z + k + NZ) % NZ) * 2 + yh, "node": node}

    partner = {"dp": z * 2 + 1 - yh, "node": node}
    sibling = {"dp": dp, "node": node + 1 - 2 * core}
    up, down = at_z(1), at_z(-1)

    def send(src, dst, ss, rs, to):
        return pltpu.make_async_remote_copy(
            src_ref=src, dst_ref=dst, send_sem=ss, recv_sem=rs, device_id=to, device_id_type=MESH
        )

    def og_copy(n):
        m = (n + 1) // 2
        t = 8 - m
        d = (z + jnp.where(n % 2 == 1, t, NZ - t)) % NZ
        return pltpu.make_async_copy(
            og.at[:, pl.ds(pl.multiple_of(d * WIDE, WIDE), WIDE)], ogv.at[n], og_sem.at[n]
        )

    def og_start(n, carry):
        og_copy(n).start()
        return carry

    tok_copy = pltpu.make_async_copy(tok_in, tok, in_sem.at[0])
    tok_copy.start()
    for n in range(3):
        og_copy(n).start()
    barrier = pltpu.get_barrier_semaphore()
    for to in (up, down):
        pl.semaphore_signal(barrier, inc=1, device_id=to, device_id_type=MESH)

    def greet(k, carry):
        other = (node + k) % NODE
        pl.semaphore_signal(barrier, inc=1, device_id={"dp": z * 2 + 1 - yh, "node": other}, device_id_type=MESH)

        @pl.when(k > 0)
        def _():
            pl.semaphore_signal(barrier, inc=1, device_id={"dp": dp, "node": other}, device_id_type=MESH)

        return carry

    lax.fori_loop(0, NODE, greet, 0)
    moves = jnp.logical_not((node == z) & (chip == z) & (core == yh))

    @pl.when(moves)
    def _():
        pl.semaphore_signal(
            barrier, inc=1, device_id={"dp": chip * 2 + core, "node": z}, device_id_type=MESH
        )

    lax.fori_loop(3, NZ, og_start, 0)
    tok_copy.wait()
    mine = pl.multiple_of(yh * HALF, HALF)
    theirs = pl.multiple_of((1 - yh) * HALF, HALF)
    for c in range(4):
        rows = slice(c * 256, (c + 1) * 256)
        tokt[:HALF, rows] = tok[rows, pl.ds(mine, HALF)].T
        tokt[HALF:, rows] = tok[rows, pl.ds(theirs, HALF)].T
    pl.semaphore_wait(barrier, jnp.where(moves, 34, 33))

    def y_copy(n):
        return send(ysend.at[n], yrecv.at[n], y_s.at[n], y_r.at[n], partner)


    def partial(n, carry):
        og_copy(n).wait()
        block = dot(tokt[...], ogv[n])
        ysend[n] = block[HALF:, :].astype(BF16)
        y_copy(n).start()
        keep[n] = block[:HALF, :]
        return carry

    def z_copy(d, t, s):
        rows = pl.ds(s * PART, PART)
        return send(
            zsend.at[d, t - 1, rows], zrecv.at[d, t - 1, rows], z_s.at[d, t - 1, s], z_r.at[d, t - 1, s],
            up if d == 0 else down,
        )

    def z_has(d, t, s):
        return t < 8 or s // (PARTS // 2) == d

    def z_stage(t):
        for s in range(PARTS):
            for d in range(2):
                if not z_has(d, t, s):
                    continue
                n = 0 if t == 8 else 2 * (8 - t) - 1 + d
                if s == 0:
                    y_copy(n).wait_recv()
                rows = pl.ds(s * PART, PART)
                value = keep[n, rows, :] + yrecv[n, rows, :].astype(F32)
                if t < 8 and z_has(d, t + 1, s):
                    z_copy(d, t + 1, s).wait_recv()
                    value = value + zrecv[d, t, rows, :]
                zsend[d, t - 1, rows, :] = value
                z_copy(d, t, s).start()

    def z_wait_send(t):
        for s in range(PARTS):
            for d in range(2):
                if z_has(d, t, s):
                    z_copy(d, t, s).wait_send()

    lax.fori_loop(0, 7, partial, 0)
    z_stage(8)
    lax.fori_loop(7, 10, partial, 0)
    z_stage(7)
    lax.fori_loop(10, 13, partial, 0)
    z_stage(6)
    lax.fori_loop(13, 16, partial, 0)
    for t in range(5, 0, -1):
        z_stage(t)
    y_copy(15).wait_recv()
    for s in range(PARTS):
        rows = pl.ds(s * PART, PART)
        value = keep[15, rows, :] + yrecv[15, rows, :].astype(F32)
        for d in range(2):
            z_copy(d, 1, s).wait_recv()
            value = value + zrecv[d, 0, rows, :]
        ga[0, rows, :] = value.astype(BF16)

    def a_has(d, k, s):
        return k < 8 or s == d

    def a_copy(d, k, s):
        rows = pl.ds(s * SUB, SUB)
        src, dst = ((NZ - k + 1) % NZ, NZ - k) if d == 0 else (k - 1, k)
        return send(
            ga.at[src, rows], ga.at[dst, rows], a_s.at[d, k - 1, s], a_r.at[d, k - 1, s], up if d == 0 else down
        )

    def c_copy(r):
        return send(ga.at[r, pl.ds(0, HALF)], ga.at[r, pl.ds(HALF, HALF)], c_s.at[r], c_r.at[r], sibling)

    def a_start(k):
        for s in range(2):
            for d in range(2):
                if k > 1 and a_has(d, k - 1, s):
                    a_copy(d, k - 1, s).wait_recv()
                if k < 9 and a_has(d, k, s):
                    a_copy(d, k, s).start()

    own = (chip - z + NZ) % NZ
    stays = (node == z) & (chip == z) & (core == yh)

    def t_copy():
        return send(
            ga.at[0, pl.ds(0, HALF)], bz.at[(z - node + NZ) % NZ], t_s.at[0], b_r.at[(z - node + NZ) % NZ],
            {"dp": node * 2 + z // 8, "node": (z % 8) * 2 + yh},
        )

    def b_here(r):
        return send(bz.at[r], bz.at[r], t_s.at[0], b_r.at[r], partner)

    def b_copy(k):
        to = (chip + k) % NZ
        return send(
            bz.at[own], bz.at[own], b_s.at[k - 1], b_r.at[own], {"dp": z * 2 + to // 8, "node": (to % 8) * 2 + core}
        )

    def left_spread(low, high):
        far = jnp.minimum(own, NZ - own)

        @pl.when((far >= low) & (far <= high))
        def _():
            @pl.when(jnp.logical_not(stays))
            def _():
                b_here(own).wait_recv()

            def go(k, carry):
                b_copy(k).start()
                return carry

            lax.fori_loop(1, NZ, go, 0)

    def left_dot(groups):
        tiles = [r for g in groups for r in group(g)]
        for r in tiles:
            @pl.when(own != r)
            def _():
                b_here(r).wait_recv()

        value = lacc[...] if tiles[0] != 0 else None
        for r in tiles:
            term = dot_t(ga[r], bz[r])
            value = term if value is None else value + term
        lacc[...] = value

    def r_copy(r):
        return send(
            rsend.at[r], rrecv.at[chip], r_s.at[r], r_r.at[chip], {"dp": z * 2 + core, "node": (z + r) % NZ}
        )

    def r_self(r):
        return (yh == core) & (node == (z + r) % NZ)

    def right_dot(r):
        value = dot(at[...], ga[r]).astype(BF16)

        @pl.when(r_self(r))
        def _():
            rrecv[chip] = value

        @pl.when(jnp.logical_not(r_self(r)))
        def _():
            rsend[r] = value
            r_copy(r).start()

    a_start(1)
    c_copy(0).start()

    @pl.when(stays)
    def _():
        bz[0] = ga[0, :HALF, :]

    @pl.when(jnp.logical_not(stays))
    def _():
        t_copy().start()

    slab = pl.ds(pl.multiple_of(core * HALF, HALF), HALF)
    c_copy(0).wait_recv()
    at[...] = ga[0, :, slab].astype(F32).T.astype(BF16)
    def drain(n, carry):
        y_copy(n).wait_send()
        return carry

    right_at = {5: (0, 1, 2), 6: (3, 4, 5), 7: (6, 7), 8: (8,)}
    for step in range(1, 9):
        a_start(step + 1)
        for r in group(step):
            c_copy(r).start()
        if step == 1:
            z_wait_send(8)
            z_wait_send(7)
            lax.fori_loop(0, NZ, drain, 0)
        if step == 2:
            left_spread(0, 2)
        if step == 3:
            left_spread(3, 5)
        if step == 4:
            left_spread(6, 8)
        for r in group(step):
            c_copy(r).wait_recv()
        for g in right_at.get(step, ()):
            for r in group(g):
                right_dot(r)
        if step == 7:
            left_dot((0, 1, 2))
        if step in (1, 2, 3):
            z_wait_send(8 - 2 * step)
            z_wait_send(7 - 2 * step)
    left_dot((3, 4, 5))
    left_dot((6, 7, 8))

    def f_copy(j):
        return send(
            lacc.at[pl.ds(j * HALF, HALF)], lrecv.at[yh], f_s.at[j], f_r.at[yh],
            {"dp": z * 2 + core, "node": node if j == 0 else node + 1 - 2 * core},
        )

    def f_here(h):
        return send(lrecv.at[h], lrecv.at[h], f_s.at[0], f_r.at[h], partner)

    f_copy(1).start()

    @pl.when(yh == core)
    def _():
        lrecv[yh] = lacc[:HALF, :]

    @pl.when(yh != core)
    def _():
        f_copy(0).start()

    for k in range(1, 9):
        for s in range(2):
            for d in range(2):
                if a_has(d, k, s):
                    a_copy(d, k, s).wait_send()

    @pl.when(jnp.logical_not(stays))
    def _():
        t_copy().wait_send()

    def b_drain(k, carry):
        b_copy(k).wait_send()
        return carry

    lax.fori_loop(1, NZ, b_drain, 0)
    for r in range(NZ):
        c_copy(r).wait_send()

    def r_here(i):
        return send(rrecv.at[i], rrecv.at[i], r_s.at[0], r_r.at[i], partner)

    total = None
    for i in range(NZ):
        @pl.when(jnp.logical_not((core == yh) & (chip == i)))
        def _():
            r_here(i).wait_recv()

        piece = rrecv[i].astype(F32)
        total = piece if total is None else total + piece
    rout[...] = total.T
    for h in range(2):
        @pl.when(jnp.logical_not((core == yh) & (yh == h)))
        def _():
            f_here(h).wait_recv()

        rows = slice(h * HALF, (h + 1) * HALF)
        lout[rows, :] = lrecv[h]

    f_copy(1).wait_send()

    @pl.when(yh != core)
    def _():
        f_copy(0).wait_send()

    for r in range(NZ):
        @pl.when(jnp.logical_not(r_self(r)))
        def _():
            r_copy(r).wait_send()


def shards(tokens_in, out_grads, left_old, right_old):
    dma = pltpu.SemaphoreType.DMA
    vmem = pl.BlockSpec(memory_space=pltpu.VMEM)
    left_new, right_new = pl.pallas_call(
        kernel,
        out_shape=(jax.ShapeDtypeStruct((BAND, HALF), F32),) * 2,
        in_specs=[pl.BlockSpec(memory_space=pl.ANY)] * 2,
        out_specs=(vmem, vmem),
        scratch_shapes=[
            pltpu.VMEM((TOK, BAND), BF16),
            pltpu.VMEM((BAND, TOK), BF16),
            pltpu.VMEM((NZ, TOK, WIDE), BF16),
            pltpu.VMEM((NZ, HALF, WIDE), F32),
            pltpu.VMEM((NZ, HALF, WIDE), BF16),
            pltpu.VMEM((NZ, HALF, WIDE), BF16),
            pltpu.VMEM((2, 8, HALF, WIDE), F32),
            pltpu.VMEM((2, 8, HALF, WIDE), F32),
            pltpu.VMEM((NZ, BAND, WIDE), BF16),
            pltpu.VMEM((HALF, BAND), BF16),
            pltpu.VMEM((NZ, HALF, WIDE), BF16),
            pltpu.VMEM((NZ, HALF, WIDE), BF16),
            pltpu.VMEM((NZ, HALF, WIDE), BF16),
            pltpu.VMEM((BAND, HALF), F32),
            pltpu.VMEM((2, HALF, HALF), F32),
            dma((1,)), dma((NZ,)), dma((NZ,)), dma((NZ,)),
            dma((2, 8, PARTS)), dma((2, 8, PARTS)),
            dma((2, 8, 2)), dma((2, 8, 2)),
            dma((NZ,)), dma((NZ,)),
            dma((NZ,)), dma((NZ,)),
            dma((1,)), dma((NZ - 1,)), dma((NZ,)),
            dma((2,)), dma((2,)),
        ],
        compiler_params=pltpu.CompilerParams(
            collective_id=0, has_side_effects=True, vmem_limit_bytes=60 * 2**20
        ),
        cost_estimate=pl.CostEstimate(flops=2 * TOK * BAND * 4096, bytes_accessed=TOK * 4096 * 2, transcendentals=0),
    )(tokens_in, out_grads)
    left_out = decay * left_old + (1.0 - decay) * left_new
    right_out = decay * right_old + (1.0 - decay) * right_new
    return left_out, right_out


def solution(mesh):
    return jax.shard_map(
        shards,
        mesh=mesh,
        in_specs=(P("dp", "node"), P("dp", None), P("node", "dp"), P("node", "dp")),
        out_specs=(P("node", "dp"), P("node", "dp")),
        check_vma=False,
    )
```

```python
import jax
import jax.numpy as jnp
from jax import lax
from jax.experimental import pallas as pl
from jax.experimental.pallas import tpu as pltpu
from jax.sharding import PartitionSpec as P

MESH = pl.DeviceIdType.MESH
F32, BF16 = jnp.float32, jnp.bfloat16
decay = 0.95
NZ, NODE = 16, 16
TOK, BAND, WIDE, HALF, SUB = 1024, 256, 256, 128, 64
PARTS = 4
PART = HALF // PARTS


def dot(a, b):
    return lax.dot_general(a, b, (((1,), (0,)), ((), ())), preferred_element_type=F32)


def dot_t(a, b):
    return lax.dot_general(a, b, (((1,), (1,)), ((), ())), preferred_element_type=F32)


def group(g):
    return [0] if g == 0 else [8] if g == 8 else [g, NZ - g]


def kernel(
    tok_in, og, lout, rout,
    tok, tokt, ogv, keep, ysend, yrecv, zsend, zrecv, ga, at, rsend, rrecv, bz, lacc, lrecv,
    in_sem, og_sem, y_s, y_r, z_s, z_r, a_s, a_r, c_s, c_r, r_s, r_r, t_s, b_s, b_r, f_s, f_r,
):
    dp, node = lax.axis_index("dp"), lax.axis_index("node")
    z, yh = dp // 2, dp % 2
    core = node % 2
    chip = yh * 8 + node // 2

    def at_z(k):
        return {"dp": ((z + k + NZ) % NZ) * 2 + yh, "node": node}

    partner = {"dp": z * 2 + 1 - yh, "node": node}
    sibling = {"dp": dp, "node": node + 1 - 2 * core}
    up, down = at_z(1), at_z(-1)

    def send(src, dst, ss, rs, to):
        return pltpu.make_async_remote_copy(
            src_ref=src, dst_ref=dst, send_sem=ss, recv_sem=rs, device_id=to, device_id_type=MESH
        )

    def og_copy(n):
        m = (n + 1) // 2
        t = 8 - m
        d = (z + jnp.where(n % 2 == 1, t, NZ - t)) % NZ
        return pltpu.make_async_copy(
            og.at[:, pl.ds(pl.multiple_of(d * WIDE, WIDE), WIDE)], ogv.at[n], og_sem.at[n]
        )

    def og_start(n, carry):
        og_copy(n).start()
        return carry

    tok_copy = pltpu.make_async_copy(tok_in, tok, in_sem.at[0])
    tok_copy.start()
    for n in range(3):
        og_copy(n).start()
    barrier = pltpu.get_barrier_semaphore()
    for to in (up, down):
        pl.semaphore_signal(barrier, inc=1, device_id=to, device_id_type=MESH)

    def greet(k, carry):
        other = (node + k) % NODE
        pl.semaphore_signal(barrier, inc=1, device_id={"dp": z * 2 + 1 - yh, "node": other}, device_id_type=MESH)

        @pl.when(k > 0)
        def _():
            pl.semaphore_signal(barrier, inc=1, device_id={"dp": dp, "node": other}, device_id_type=MESH)

        return carry

    lax.fori_loop(0, NODE, greet, 0)
    moves = jnp.logical_not((node == z) & (chip == z) & (core == yh))

    @pl.when(moves)
    def _():
        pl.semaphore_signal(
            barrier, inc=1, device_id={"dp": chip * 2 + core, "node": z}, device_id_type=MESH
        )

    lax.fori_loop(3, NZ, og_start, 0)
    tok_copy.wait()
    mine = pl.multiple_of(yh * HALF, HALF)
    theirs = pl.multiple_of((1 - yh) * HALF, HALF)
    for c in range(4):
        rows = slice(c * 256, (c + 1) * 256)
        tokt[:HALF, rows] = tok[rows, pl.ds(mine, HALF)].T
        tokt[HALF:, rows] = tok[rows, pl.ds(theirs, HALF)].T
    pl.semaphore_wait(barrier, jnp.where(moves, 34, 33))

    def y_copy(n):
        return send(ysend.at[n], yrecv.at[n], y_s.at[n], y_r.at[n], partner)


    def partial(n, carry):
        og_copy(n).wait()
        block = dot(tokt[...], ogv[n])
        ysend[n] = block[HALF:, :].astype(BF16)
        y_copy(n).start()
        keep[n] = block[:HALF, :]
        return carry

    def z_copy(d, t, s):
        rows = pl.ds(s * PART, PART)
        return send(
            zsend.at[d, t - 1, rows], zrecv.at[d, t - 1, rows], z_s.at[d, t - 1, s], z_r.at[d, t - 1, s],
            up if d == 0 else down,
        )

    def z_has(d, t, s):
        return t < 8 or s // (PARTS // 2) == d

    def z_stage(t):
        for s in range(PARTS):
            for d in range(2):
                if not z_has(d, t, s):
                    continue
                n = 0 if t == 8 else 2 * (8 - t) - 1 + d
                if s == 0:
                    y_copy(n).wait_recv()
                rows = pl.ds(s * PART, PART)
                value = keep[n, rows, :] + yrecv[n, rows, :].astype(F32)
                if t < 8 and z_has(d, t + 1, s):
                    z_copy(d, t + 1, s).wait_recv()
                    value = value + zrecv[d, t, rows, :]
                zsend[d, t - 1, rows, :] = value
                z_copy(d, t, s).start()

    def z_wait_send(t):
        for s in range(PARTS):
            for d in range(2):
                if z_has(d, t, s):
                    z_copy(d, t, s).wait_send()

    lax.fori_loop(0, 7, partial, 0)
    z_stage(8)
    lax.fori_loop(7, 10, partial, 0)
    z_stage(7)
    lax.fori_loop(10, 13, partial, 0)
    z_stage(6)
    lax.fori_loop(13, 16, partial, 0)
    for t in range(5, 0, -1):
        z_stage(t)
    y_copy(15).wait_recv()
    for s in range(PARTS):
        rows = pl.ds(s * PART, PART)
        value = keep[15, rows, :] + yrecv[15, rows, :].astype(F32)
        for d in range(2):
            z_copy(d, 1, s).wait_recv()
            value = value + zrecv[d, 0, rows, :]
        ga[0, rows, :] = value.astype(BF16)

    def a_has(d, k, s):
        return k < 8 or s == d

    def a_copy(d, k, s):
        rows = pl.ds(s * SUB, SUB)
        src, dst = ((NZ - k + 1) % NZ, NZ - k) if d == 0 else (k - 1, k)
        return send(
            ga.at[src, rows], ga.at[dst, rows], a_s.at[d, k - 1, s], a_r.at[d, k - 1, s], up if d == 0 else down
        )

    def c_copy(r):
        return send(ga.at[r, pl.ds(0, HALF)], ga.at[r, pl.ds(HALF, HALF)], c_s.at[r], c_r.at[r], sibling)

    def a_start(k):
        for s in range(2):
            for d in range(2):
                if k > 1 and a_has(d, k - 1, s):
                    a_copy(d, k - 1, s).wait_recv()
                if k < 9 and a_has(d, k, s):
                    a_copy(d, k, s).start()

    own = (chip - z + NZ) % NZ
    stays = (node == z) & (chip == z) & (core == yh)

    def t_copy():
        return send(
            ga.at[0, pl.ds(0, HALF)], bz.at[(z - node + NZ) % NZ], t_s.at[0], b_r.at[(z - node + NZ) % NZ],
            {"dp": node * 2 + z // 8, "node": (z % 8) * 2 + yh},
        )

    def b_here(r):
        return send(bz.at[r], bz.at[r], t_s.at[0], b_r.at[r], partner)

    def b_copy(k):
        to = (chip + k) % NZ
        return send(
            bz.at[own], bz.at[own], b_s.at[k - 1], b_r.at[own], {"dp": z * 2 + to // 8, "node": (to % 8) * 2 + core}
        )

    def left_spread(low, high):
        far = jnp.minimum(own, NZ - own)

        @pl.when((far >= low) & (far <= high))
        def _():
            @pl.when(jnp.logical_not(stays))
            def _():
                b_here(own).wait_recv()

            def go(k, carry):
                b_copy(k).start()
                return carry

            lax.fori_loop(1, NZ, go, 0)

    def left_dot(groups):
        tiles = [r for g in groups for r in group(g)]
        for r in tiles:
            @pl.when(own != r)
            def _():
                b_here(r).wait_recv()

        value = lacc[...] if tiles[0] != 0 else None
        for r in tiles:
            term = dot_t(ga[r], bz[r])
            value = term if value is None else value + term
        lacc[...] = value

    def r_copy(r):
        return send(
            rsend.at[r], rrecv.at[chip], r_s.at[r], r_r.at[chip], {"dp": z * 2 + core, "node": (z + r) % NZ}
        )

    def r_self(r):
        return (yh == core) & (node == (z + r) % NZ)

    def right_dot(r):
        value = dot(at[...], ga[r]).astype(BF16)

        @pl.when(r_self(r))
        def _():
            rrecv[chip] = value

        @pl.when(jnp.logical_not(r_self(r)))
        def _():
            rsend[r] = value
            r_copy(r).start()

    @pl.when(jnp.logical_not(stays))
    def _():
        t_copy().start()

    a_start(1)
    c_copy(0).start()

    @pl.when(stays)
    def _():
        bz[0] = ga[0, :HALF, :]

    slab = pl.ds(pl.multiple_of(core * HALF, HALF), HALF)
    c_copy(0).wait_recv()
    at[...] = ga[0, :, slab].astype(F32).T.astype(BF16)
    def drain(n, carry):
        y_copy(n).wait_send()
        return carry

    right_at = {5: (0, 1, 2), 6: (3, 4, 5), 7: (6, 7), 8: (8,)}
    for step in range(1, 9):
        a_start(step + 1)
        for r in group(step):
            c_copy(r).start()
        if step == 1:
            z_wait_send(8)
            z_wait_send(7)
            lax.fori_loop(0, NZ, drain, 0)
        if step == 2:
            left_spread(0, 2)
        if step == 3:
            left_spread(3, 5)
        if step == 4:
            left_spread(6, 8)
        for r in group(step):
            c_copy(r).wait_recv()
        for g in right_at.get(step, ()):
            for r in group(g):
                right_dot(r)
        if step == 7:
            left_dot((0, 1, 2))
        if step in (1, 2, 3):
            z_wait_send(8 - 2 * step)
            z_wait_send(7 - 2 * step)
    left_dot((3, 4, 5))
    left_dot((6, 7, 8))

    def f_copy(j):
        return send(
            lacc.at[pl.ds(j * HALF, HALF)], lrecv.at[yh], f_s.at[j], f_r.at[yh],
            {"dp": z * 2 + core, "node": node if j == 0 else node + 1 - 2 * core},
        )

    def f_here(h):
        return send(lrecv.at[h], lrecv.at[h], f_s.at[0], f_r.at[h], partner)

    f_copy(1).start()

    @pl.when(yh == core)
    def _():
        lrecv[yh] = lacc[:HALF, :]

    @pl.when(yh != core)
    def _():
        f_copy(0).start()

    for k in range(1, 9):
        for s in range(2):
            for d in range(2):
                if a_has(d, k, s):
                    a_copy(d, k, s).wait_send()

    @pl.when(jnp.logical_not(stays))
    def _():
        t_copy().wait_send()

    def b_drain(k, carry):
        b_copy(k).wait_send()
        return carry

    lax.fori_loop(1, NZ, b_drain, 0)
    for r in range(NZ):
        c_copy(r).wait_send()

    def r_here(i):
        return send(rrecv.at[i], rrecv.at[i], r_s.at[0], r_r.at[i], partner)

    total = None
    for i in range(NZ):
        @pl.when(jnp.logical_not((core == yh) & (chip == i)))
        def _():
            r_here(i).wait_recv()

        piece = rrecv[i].astype(F32)
        total = piece if total is None else total + piece
    rout[...] = total.T
    for h in range(2):
        @pl.when(jnp.logical_not((core == yh) & (yh == h)))
        def _():
            f_here(h).wait_recv()

        rows = slice(h * HALF, (h + 1) * HALF)
        lout[rows, :] = lrecv[h]

    f_copy(1).wait_send()

    @pl.when(yh != core)
    def _():
        f_copy(0).wait_send()

    for r in range(NZ):
        @pl.when(jnp.logical_not(r_self(r)))
        def _():
            r_copy(r).wait_send()


def shards(tokens_in, out_grads, left_old, right_old):
    dma = pltpu.SemaphoreType.DMA
    vmem = pl.BlockSpec(memory_space=pltpu.VMEM)
    left_new, right_new = pl.pallas_call(
        kernel,
        out_shape=(jax.ShapeDtypeStruct((BAND, HALF), F32),) * 2,
        in_specs=[pl.BlockSpec(memory_space=pl.ANY)] * 2,
        out_specs=(vmem, vmem),
        scratch_shapes=[
            pltpu.VMEM((TOK, BAND), BF16),
            pltpu.VMEM((BAND, TOK), BF16),
            pltpu.VMEM((NZ, TOK, WIDE), BF16),
            pltpu.VMEM((NZ, HALF, WIDE), F32),
            pltpu.VMEM((NZ, HALF, WIDE), BF16),
            pltpu.VMEM((NZ, HALF, WIDE), BF16),
            pltpu.VMEM((2, 8, HALF, WIDE), F32),
            pltpu.VMEM((2, 8, HALF, WIDE), F32),
            pltpu.VMEM((NZ, BAND, WIDE), BF16),
            pltpu.VMEM((HALF, BAND), BF16),
            pltpu.VMEM((NZ, HALF, WIDE), BF16),
            pltpu.VMEM((NZ, HALF, WIDE), BF16),
            pltpu.VMEM((NZ, HALF, WIDE), BF16),
            pltpu.VMEM((BAND, HALF), F32),
            pltpu.VMEM((2, HALF, HALF), F32),
            dma((1,)), dma((NZ,)), dma((NZ,)), dma((NZ,)),
            dma((2, 8, PARTS)), dma((2, 8, PARTS)),
            dma((2, 8, 2)), dma((2, 8, 2)),
            dma((NZ,)), dma((NZ,)),
            dma((NZ,)), dma((NZ,)),
            dma((1,)), dma((NZ - 1,)), dma((NZ,)),
            dma((2,)), dma((2,)),
        ],
        compiler_params=pltpu.CompilerParams(
            collective_id=0, has_side_effects=True, vmem_limit_bytes=60 * 2**20
        ),
        cost_estimate=pl.CostEstimate(flops=2 * TOK * BAND * 4096, bytes_accessed=TOK * 4096 * 2, transcendentals=0),
    )(tokens_in, out_grads)
    left_out = decay * left_old + (1.0 - decay) * left_new
    right_out = decay * right_old + (1.0 - decay) * right_new
    return left_out, right_out


def solution(mesh):
    return jax.shard_map(
        shards,
        mesh=mesh,
        in_specs=(P("dp", "node"), P("dp", None), P("node", "dp"), P("node", "dp")),
        out_specs=(P("node", "dp"), P("node", "dp")),
        check_vma=False,
    )
```
